256 devices in a mesh: row: 8 (over x, core), col: 32 (over y, z).
Axes of the slice: x: 4, y: 4, z: 8, core: 2. Of those that a mesh axis runs over, the one named last changes fastest.
Arguments:
- covariance: float32 [8, 2048, 2, 8192], P(None, 'row', None, 'col'), may hold values from 0 to 5, as said below
Outputs:
- factored: float32 [8, 2048, 2, 8192], P(None, 'row', None, 'col')
The draws below stay inside these ranges and needn't reach their ends.
Inputs may be any that keep to these rules, and one draw needn't show every extreme that they name: covariance is symmetric positive definite: s_a s_b m(d_ab) plus a positive nugget on the diagonal, where m is the Matern 3/2 kernel of the distance d_ab between two units' feature points.
All inputs are finite; a program needn't handle non-finite values.
Results may differ from the reference program's by a relative error of at most 0.0001.
Values sent between devices are 32-bit elements; how exact they have to be, the bound alone decides.
No kernel may reach another device: no remote copies, remote signals or barrier semaphores. Data moves between devices by JAX's collectives and lax.ppermute only.
A program may use at most 128 MiB of HBM per device.

```python
import jax
import jax.numpy as jnp
from jax import lax

B = 256
TC = 2
STEPS = 3
TR = 8
ORDER = 16384


def draw_covariance(key, part):
    keys = jax.random.split(key, 3)
    points = jax.random.uniform(keys[0], (ORDER, 3), jnp.float32)
    length = 0.25
    scales = jnp.exp(jax.random.uniform(keys[1], (ORDER,), jnp.float32, jnp.log(0.7), jnp.log(1.4)))
    nugget = jnp.exp(jax.random.uniform(keys[2], (ORDER,), jnp.float32, jnp.log(0.3), jnp.log(1.0)))
    squared = jnp.zeros((ORDER, ORDER), jnp.float32)
    for coord in range(3):
        spread = points[:, coord][:, None] - points[:, coord][None, :]
        squared = squared + spread * spread
    rescaled_block = jnp.sqrt(3.0) * jnp.sqrt(squared) / length
    kernel = (1.0 + rescaled_block) * jnp.exp(-rescaled_block)
    covariance_matrix = scales[:, None] * scales[None, :] * kernel + jnp.diag(nugget)
    return covariance_matrix.reshape(TR, ORDER // TR, TC, ORDER // TC)


def setup_inputs(seed: int = 0) -> dict:
    arg_keys = jax.random.split(jax.random.key(seed), 2)
    covariance = draw_covariance(jax.random.fold_in(arg_keys[1], 71), 0)
    return {"covariance": covariance}


def reference(covariance):
    covariance_matrix = covariance.reshape(ORDER, ORDER)
    tile_index = (jnp.arange(ORDER, dtype=jnp.int32) // B).astype(jnp.int32)
    identity = jnp.eye(B, dtype=jnp.float32)
    for k in range(STEPS):
        first = k * B
        last = first + B
        factor = jnp.linalg.cholesky(covariance_matrix[first:last, first:last])
        inverted_factor = jax.scipy.linalg.solve_triangular(factor, identity, lower=True)
        panel = jnp.dot(covariance_matrix[last:, first:last], inverted_factor.T, precision=lax.Precision.HIGHEST)
        trailing = covariance_matrix[last:, last:]
        refreshed_block = trailing - jnp.dot(panel, panel.T, precision=lax.Precision.HIGHEST)
        tiles = tile_index[last:]
        keep = tiles[:, None] >= tiles[None, :]
        covariance_matrix = covariance_matrix.at[last:, last:].set(jnp.where(keep, refreshed_block, trailing))
        covariance_matrix = covariance_matrix.at[last:, first:last].set(panel)
        covariance_matrix = covariance_matrix.at[first:last, first:last].set(factor)
    return covariance_matrix.reshape(TR, ORDER // TR, TC, ORDER // TC)
```

```python
import functools

import jax
import jax.numpy as jnp
from jax import lax
from jax.experimental import pallas as pl
from jax.experimental.pallas import tpu as pltpu
from jax.sharding import PartitionSpec as P

B = 256
BAND = 32
PIV = 4
PAIRS = tuple((k, j) for k in range(3) for j in range(k, 3))
HIGHEST = lax.Precision.HIGHEST
F32 = jnp.float32
BF16 = jnp.bfloat16


def dot(a, b):
    return jnp.dot(a, b, precision=HIGHEST, preferred_element_type=F32)


def dot_tn(a, b):
    return lax.dot_general(
        a, b, (((0,), (0,)), ((), ())), precision=HIGHEST, preferred_element_type=F32
    )


def split(a):
    hi = a.astype(BF16)
    return hi, (a - hi.astype(F32)).astype(BF16)


def band_eliminate(rows, band):
    iota = lax.broadcasted_iota(jnp.int32, (8, 128), 0)
    chunks = list(rows[0].keys())
    groups = BAND // 8
    for g in range(0, BAND, PIV):
        mine, first = g // 8, g % 8
        col = band * BAND + g
        piv_chunk, lane = col // 128, col % 128
        v = [
            [
                jnp.broadcast_to(rows[s][piv_chunk][:, lane + a : lane + a + 1], (8, 128)) if s >= mine else None
                for s in range(groups)
            ]
            for a in range(PIV)
        ]
        row = [
            {c: jnp.broadcast_to(rows[mine][c][first + a : first + a + 1, :], (8, 128)) for c in chunks}
            for a in range(PIV)
        ]
        s = {
            (a, b): jnp.broadcast_to(v[b][mine][first + a : first + a + 1, :], (8, 128))
            for a in range(PIV)
            for b in range(a, PIV)
        }
        inv, root = [], []
        for a in range(PIV):
            inv.append(1.0 / s[a, a])
            root.append(lax.rsqrt(s[a, a]))
            for b in range(a + 1, PIV):
                ratio = s[a, b] * inv[a]
                for c in range(b, PIV):
                    s[b, c] = s[b, c] - ratio * s[a, c]
                for c in chunks:
                    row[b][c] = row[b][c] - ratio * row[a][c]
                for h in range(mine, groups):
                    v[b][h] = v[b][h] - ratio * v[a][h]
        for h in range(mine, groups):
            if h == mine and first + PIV == 8:
                continue
            scaled = [v[a][h] * inv[a] for a in range(PIV)]
            for c in chunks:
                total = scaled[0] * row[0][c]
                for a in range(1, PIV):
                    total = total + scaled[a] * row[a][c]
                new = rows[h][c] - total
                rows[h][c] = jnp.where(iota >= first + PIV, new, rows[h][c]) if h == mine else new
        for a in range(PIV):
            for c in chunks:
                rows[mine][c] = jnp.where(iota == first + a, row[a][c] * root[a], rows[mine][c])
    return rows


def factor_tile(g_ref):
    for band in range(B // BAND):
        lo = band * BAND
        chunks = (0, 1, 2) if band < 4 else (1, 2, 3)
        rows = [
            {c: g_ref[lo + 8 * s : lo + 8 * s + 8, 128 * c : 128 * c + 128] for c in chunks}
            for s in range(BAND // 8)
        ]
        rows = band_eliminate(rows, band)
        for s in range(BAND // 8):
            for c in chunks:
                g_ref[lo + 8 * s : lo + 8 * s + 8, 128 * c : 128 * c + 128] = rows[s][c]
        hi = lo + BAND
        if hi < B:
            left, right = 128 * chunks[0], 128 * chunks[-1] + 128
            done = g_ref[lo:hi, left:right]
            turned = g_ref[lo:hi, 0:B].T
            g_ref[hi : hi + BAND, left:right] -= dot(turned[hi : hi + BAND], done)
            if hi + BAND < B:
                g_ref[hi + BAND : B, left:right] -= dot(turned[hi + BAND : B], done)


def factor_kernel(place_ref, *refs):
    own, other = refs[0:4], refs[4:8]
    panel_ref, zhi_ref, zlo_ref, diag_ref, t_ref, g_ref, v_ref, lt_ref = refs[8:]
    my_row, my_col = place_ref[0], place_ref[1]
    x, core = my_row // 2, my_row % 2
    y = my_col // 8
    for shift in range(4):
        for side, bufs in ((core, own), (1 - core, other)):
            base = (((x - shift + 4) % 4) * 2 + side) * 32
            for step in range(4):
                at = pl.multiple_of(base + ((y - step + 4) % 4) * 8, 8)
                for n, (k, j) in enumerate(PAIRS):
                    t_ref[k, pl.ds(at, 8), j * B : (j + 1) * B] = bufs[shift][step, n]
    for p in range(8):
        for k in range(3):
            t_ref[k, p * 32 : p * 32 + 32, 3 * B :] = panel_ref[p, k]
    identity = jnp.where(
        lax.broadcasted_iota(jnp.int32, (B, B), 0) == lax.broadcasted_iota(jnp.int32, (B, B), 1), 1.0, 0.0
    ).astype(F32)
    upper = lax.broadcasted_iota(jnp.int32, (B, B), 0) <= lax.broadcasted_iota(jnp.int32, (B, B), 1)

    def step(k, carry):
        for j in range(3):

            @pl.when(k == j)
            def _():
                g_ref[:, 0:B] = t_ref[j, :, j * B : (j + 1) * B]

        g_ref[:, B:] = identity
        factor_tile(g_ref)
        lt_ref[k] = jnp.where(upper, g_ref[:, 0:B], 0.0)
        v_ref[k] = g_ref[:, B:]
        for j in range(3):

            @pl.when(k == j)
            def _():
                lo = (j + 1) * B
                solved = dot(v_ref[j], t_ref[j, :, lo:])
                t_ref[j, :, lo:] = solved
                for i in range(j + 1, 3):
                    t_ref[i, :, i * B :] -= dot_tn(
                        t_ref[j, :, i * B : (i + 1) * B], t_ref[j, :, i * B :]
                    )

        return carry

    lax.fori_loop(0, 3, step, 0)
    for k in range(3):
        t_ref[k, :, 3 * B : 4 * B] = jnp.where(
            my_col == k, -identity, jnp.where(my_col < 3, 0.0, t_ref[k, :, 3 * B : 4 * B])
        )
    for k in (2, 1, 0):
        rest = t_ref[k, :, 3 * B :]
        for i in range(k + 1, 3):
            rest -= dot(t_ref[k, :, i * B : (i + 1) * B], t_ref[i, :, 3 * B :])
        z = dot_tn(v_ref[k], rest)
        t_ref[k, :, 3 * B :] = z
        hi, lo = split(z)
        for p in range(8):
            zhi_ref[p * 96 + k * 32 : p * 96 + k * 32 + 32, :] = hi[p * 32 : p * 32 + 32]
            zlo_ref[p * 96 + k * 32 : p * 96 + k * 32 + 32, :] = lo[p * 32 : p * 32 + 32]
    diag_ref[...] = lt_ref[jnp.minimum(my_col, 2)].T


def factor(place, own, other, panel):
    vmem = pl.BlockSpec(memory_space=pltpu.VMEM)
    return pl.pallas_call(
        factor_kernel,
        out_shape=(
            jax.ShapeDtypeStruct((3 * B, 2 * B), BF16),
            jax.ShapeDtypeStruct((3 * B, 2 * B), BF16),
            jax.ShapeDtypeStruct((B, B), F32),
        ),
        in_specs=[pl.BlockSpec(memory_space=pltpu.SMEM)] + [vmem] * 9,
        out_specs=(vmem, vmem, vmem),
        scratch_shapes=[
            pltpu.VMEM((3, B, 5 * B), F32),
            pltpu.VMEM((B, 2 * B), F32),
            pltpu.VMEM((3, B, B), F32),
            pltpu.VMEM((3, B, B), F32),
        ],
        compiler_params=pltpu.CompilerParams(vmem_limit_bytes=40 * 2**20),
        name="factor_panel",
    )(place, *own, *other, panel)


def update_kernel(place_ref, a_ref, u_ref, zhi_ref, zlo_ref, diag_ref, o_ref):
    t = pl.program_id(0)
    i = t * 8 + place_ref[0]
    my_col = place_ref[1]
    o_ref[...] = a_ref[...]

    @pl.when(i >= my_col)
    def _():
        hi, lo = split(u_ref[...].reshape(3 * B, B).T)

        def product(z):
            zhi, zlo = zhi_ref[:, z], zlo_ref[:, z]
            d = functools.partial(jnp.dot, preferred_element_type=F32)
            return d(hi, zhi) + (d(hi, zlo) + d(lo, zhi))

        panel = my_col < 3
        base = jnp.where(panel, 0.0, a_ref[0, :, 0, :])
        o_ref[0, :, 0, :] = base - product(slice(0, B))

        @pl.when(i >= my_col + 32)
        def _():
            o_ref[0, :, 1, :] = a_ref[0, :, 1, :] - product(slice(B, 2 * B))

        @pl.when(jnp.logical_and(i == my_col, panel))
        def _():
            o_ref[0, :, 0, :] = diag_ref[...]


def update(place, a, u, zhi, zlo, diag):
    full = pl.BlockSpec(memory_space=pltpu.VMEM)
    return pl.pallas_call(
        update_kernel,
        grid=(8,),
        out_shape=jax.ShapeDtypeStruct(a.shape, F32),
        in_specs=[
            pl.BlockSpec(memory_space=pltpu.SMEM),
            pl.BlockSpec((1, B, 2, B), lambda t: (t, 0, 0, 0)),
            pl.BlockSpec((8, 3, 32, B), lambda t: (t % 4, 0, 0, t // 4)),
            full,
            full,
            full,
        ],
        out_specs=pl.BlockSpec((1, B, 2, B), lambda t: (t, 0, 0, 0)),
        compiler_params=pltpu.CompilerParams(vmem_limit_bytes=40 * 2**20),
        name="trailing_update",
    )(place, a, u, zhi, zlo, diag)


def spread_corner(mine, my_col):
    y, z = my_col // 8, my_col % 8
    quarter = mine.reshape(3, 4, 8, B)
    got = jnp.where(y == 0, quarter[:, 0], 0.0)
    for d in range(1, 4):
        got = got + lax.ppermute(quarter[:, d], "col", [(j, d * 8 + j) for j in range(3)])
    got = jnp.where(z < 3, got, 0.0)
    got = got + lax.ppermute(got, "col", [(h * 8 + j, h * 8 + j + 4) for h in range(4) for j in range(3)])
    stack = [got]
    for s in range(1, 4):
        pairs = [
            (h * 8 + q * 4 + j, h * 8 + q * 4 + (j + s) % 4) for h in range(4) for q in range(2) for j in range(3)
        ]
        stack.append(lax.ppermute(got, "col", pairs))
    column = []
    for j in range(3):
        at = (z - j) % 4
        pick = stack[3]
        for s in range(3):
            pick = jnp.where(at == s, stack[s], pick)
        column.append(pick)
    part = jnp.stack([column[j][k] for k, j in PAIRS])
    parts = [part]
    for s in range(1, 4):
        parts.append(lax.ppermute(part, "col", [(c, (c + 8 * s) % 32) for c in range(32)]))
    block = jnp.stack(parts)
    own = [block]
    for s in range(1, 4):
        own.append(lax.ppermute(block, "row", [(r, (r + 2 * s) % 8) for r in range(8)]))
    other = [lax.ppermute(b, "row", [(r, r ^ 1) for r in range(8)]) for b in own]
    return own, other


def on_device(covariance):
    my_row, my_col = lax.axis_index("row"), lax.axis_index("col")
    place = jnp.stack([my_row, my_col]).astype(jnp.int32)
    top = covariance[0].reshape(8, 32, 2 * B)
    mine = lax.all_to_all(top, "row", 0, 0, tiled=True)[:3]
    turned = lax.ppermute(
        mine,
        ("row", "col"),
        [(r * 32 + y * 8 + z, z * 32 + y * 8 + r) for r in range(8) for y in range(4) for z in range(8)],
    )
    rows = lax.all_gather(turned, "col")
    panel = lax.all_gather(mine, "row")
    own, other = spread_corner(mine[:, :, :B], my_col)
    zhi, zlo, diag = factor(place, own, other, panel)
    return update(place, covariance, rows, zhi, zlo, diag)


def solution(mesh):
    spec = (P(None, "row", None, "col"),)
    return jax.shard_map(on_device, mesh=mesh, in_specs=spec, out_specs=spec[0], check_vma=False)
```

```python
import functools

import jax
import jax.numpy as jnp
from jax import lax
from jax.experimental import pallas as pl
from jax.experimental.pallas import tpu as pltpu
from jax.sharding import PartitionSpec as P

B = 256
BAND = 32
PIV = 8
PAIRS = tuple((k, j) for k in range(3) for j in range(k, 3))
HIGHEST = lax.Precision.HIGHEST
F32 = jnp.float32
BF16 = jnp.bfloat16


def dot(a, b):
    return jnp.dot(a, b, precision=HIGHEST, preferred_element_type=F32)


def dot_tn(a, b):
    return lax.dot_general(
        a, b, (((0,), (0,)), ((), ())), precision=HIGHEST, preferred_element_type=F32
    )


def split(a):
    hi = a.astype(BF16)
    return hi, (a - hi.astype(F32)).astype(BF16)


def product(a, b):
    mul = functools.partial(jnp.dot, preferred_element_type=F32)
    return mul(a[0], b[0]) + (mul(a[0], b[1]) + mul(a[1], b[0]))


def band_eliminate(rows, band):
    iota = lax.broadcasted_iota(jnp.int32, (8, 128), 0)
    chunks = list(rows[0].keys())
    groups = BAND // 8
    for g in range(0, BAND, PIV):
        mine, first = g // 8, g % 8
        col = band * BAND + g
        piv_chunk, lane = col // 128, col % 128
        v = [
            [
                jnp.broadcast_to(rows[s][piv_chunk][:, lane + a : lane + a + 1], (8, 128)) if s >= mine else None
                for s in range(groups)
            ]
            for a in range(PIV)
        ]
        row = [
            {c: jnp.broadcast_to(rows[mine][c][first + a : first + a + 1, :], (8, 128)) for c in chunks}
            for a in range(PIV)
        ]
        s = {
            (a, b): jnp.broadcast_to(v[b][mine][first + a : first + a + 1, :], (8, 128))
            for a in range(PIV)
            for b in range(a, PIV)
        }
        inv, root = [], []
        for a in range(PIV):
            inv.append(1.0 / s[a, a])
            root.append(lax.rsqrt(s[a, a]))
            for b in range(a + 1, PIV):
                ratio = s[a, b] * inv[a]
                for c in range(b, PIV):
                    s[b, c] = s[b, c] - ratio * s[a, c]
                for c in chunks:
                    row[b][c] = row[b][c] - ratio * row[a][c]
                for h in range(mine, groups):
                    v[b][h] = v[b][h] - ratio * v[a][h]
        for h in range(mine, groups):
            if h == mine and first + PIV == 8:
                continue
            scaled = [v[a][h] * inv[a] for a in range(PIV)]
            for c in chunks:
                total = scaled[0] * row[0][c]
                for a in range(1, PIV):
                    total = total + scaled[a] * row[a][c]
                new = rows[h][c] - total
                rows[h][c] = jnp.where(iota >= first + PIV, new, rows[h][c]) if h == mine else new
        for a in range(PIV):
            for c in chunks:
                rows[mine][c] = jnp.where(iota == first + a, row[a][c] * root[a], rows[mine][c])
    return rows


def factor_tile(g_ref):
    for band in range(B // BAND):
        lo = band * BAND
        chunks = (0, 1, 2) if lo < 128 else (1, 2, 3)
        rows = [
            {c: g_ref[lo + 8 * s : lo + 8 * s + 8, 128 * c : 128 * c + 128] for c in chunks}
            for s in range(BAND // 8)
        ]
        rows = band_eliminate(rows, band)
        for s in range(BAND // 8):
            for c in chunks:
                g_ref[lo + 8 * s : lo + 8 * s + 8, 128 * c : 128 * c + 128] = rows[s][c]
        hi = lo + BAND
        if hi < B:
            left, right = 128 * chunks[0], 128 * chunks[-1] + 128
            done = g_ref[lo:hi, left:right]
            turned = g_ref[lo:hi, 0:B].T
            g_ref[hi : hi + BAND, left:right] -= dot(turned[hi : hi + BAND], done)
            if hi + BAND < B:
                g_ref[hi + BAND : B, left:right] -= dot(turned[hi + BAND : B], done)


def upper_mask():
    return lax.broadcasted_iota(jnp.int32, (B, B), 0) <= lax.broadcasted_iota(jnp.int32, (B, B), 1)


def unit():
    rows = lax.broadcasted_iota(jnp.int32, (B, B), 0)
    return jnp.where(rows == lax.broadcasted_iota(jnp.int32, (B, B), 1), 1.0, 0.0).astype(F32)


def factor_kernel(place_ref, *refs):
    own, other = refs[0:4], refs[4:8]
    v_ref, x_ref, diag_ref, t_ref, g_ref, lt_ref = refs[8:]
    my_row, my_col = place_ref[0], place_ref[1]
    x, core = my_row // 2, my_row % 2
    y = my_col // 8
    for shift in range(4):
        for side, bufs in ((core, own), (1 - core, other)):
            base = (((x - shift + 4) % 4) * 2 + side) * 32
            for step in range(4):
                at = pl.multiple_of(base + ((y - step + 4) % 4) * 8, 8)
                for n, (k, j) in enumerate(PAIRS):
                    t_ref[k, pl.ds(at, 8), j * B : (j + 1) * B] = bufs[shift][step, n]

    def step(k, carry):
        for j in range(3):

            @pl.when(k == j)
            def _():
                g_ref[:, 0:B] = t_ref[j, :, j * B : (j + 1) * B]

        g_ref[:, B:] = unit()
        factor_tile(g_ref)
        lt_ref[k] = jnp.where(upper_mask(), g_ref[:, 0:B], 0.0)
        v_ref[k] = g_ref[:, B:]
        for j in range(2):

            @pl.when(k == j)
            def _():
                lo = (j + 1) * B
                solved = dot(v_ref[j], t_ref[j, :, lo:])
                t_ref[j, :, lo:] = solved
                for i in range(j + 1, 3):
                    t_ref[i, :, i * B :] -= dot_tn(
                        t_ref[j, :, i * B : (i + 1) * B], t_ref[j, :, i * B :]
                    )

        return carry

    lax.fori_loop(0, 3, step, 0)
    for n, (k, j) in enumerate(((0, 1), (0, 2), (1, 2))):
        x_ref[n] = t_ref[k, :, j * B : (j + 1) * B]
    diag_ref[...] = lt_ref[jnp.minimum(my_col, 2)].T


def factor(place, own, other):
    vmem = pl.BlockSpec(memory_space=pltpu.VMEM)
    return pl.pallas_call(
        factor_kernel,
        out_shape=(
            jax.ShapeDtypeStruct((3, B, B), F32),
            jax.ShapeDtypeStruct((3, B, B), F32),
            jax.ShapeDtypeStruct((B, B), F32),
        ),
        in_specs=[pl.BlockSpec(memory_space=pltpu.SMEM)] + [vmem] * 8,
        out_specs=(vmem, vmem, vmem),
        scratch_shapes=[
            pltpu.VMEM((3, B, 3 * B), F32),
            pltpu.VMEM((B, 2 * B), F32),
            pltpu.VMEM((3, B, B), F32),
        ],
        compiler_params=pltpu.CompilerParams(vmem_limit_bytes=40 * 2**20),
        cost_estimate=pl.CostEstimate(flops=30 * 10**9, bytes_accessed=10**7, transcendentals=0),
        name="factor_corner",
    )(place, *own, *other)


def solve_kernel(place_ref, v_ref, x_ref, *refs):
    pieces = refs[:8]
    zhi_ref, zlo_ref, t_ref = refs[8:]
    my_row, my_col = place_ref[0], place_ref[1]
    x, core = my_row // 2, my_row % 2
    for n in range(8):
        source = ((x - n // 2 + 4) % 4) * 2 + (core if n % 2 == 0 else 1 - core)
        at = pl.multiple_of(source * 32, 32)
        for k in range(3):
            t_ref[k, pl.ds(at, 32), :] = pieces[n][k]
    above = {(0, 1): 0, (0, 2): 1, (1, 2): 2}
    v = [split(v_ref[k]) for k in range(3)]
    vt = [split(v_ref[k].T) for k in range(3)]
    up = {key: split(x_ref[n]) for key, n in above.items()}
    down = {key: split(x_ref[n].T) for key, n in above.items()}
    sums = [t_ref[k] for k in range(3)]
    for k in range(3):
        sums[k] = product(v[k], split(sums[k]))
        for i in range(k + 1, 3):
            sums[i] = sums[i] - product(down[k, i], split(sums[k]))
    for k in range(3):
        left = jnp.where(my_col == k, -unit(), jnp.where(my_col < 3, 0.0, sums[k][:, :B]))
        sums[k] = jnp.concatenate([left, sums[k][:, B:]], axis=1)
    done = [None] * 3
    for k in (2, 1, 0):
        rest = sums[k]
        for i in range(k + 1, 3):
            rest = rest - product(up[k, i], done[i])
        done[k] = split(product(vt[k], split(rest)))
        for ref, part in ((zhi_ref, done[k][0]), (zlo_ref, done[k][1])):
            for p in range(8):
                ref[p * 96 + k * 32 : p * 96 + k * 32 + 32, :] = part[p * 32 : p * 32 + 32]


def solve(place, v, x, pieces):
    vmem = pl.BlockSpec(memory_space=pltpu.VMEM)
    return pl.pallas_call(
        solve_kernel,
        out_shape=(
            jax.ShapeDtypeStruct((3 * B, 2 * B), BF16),
            jax.ShapeDtypeStruct((3 * B, 2 * B), BF16),
        ),
        in_specs=[pl.BlockSpec(memory_space=pltpu.SMEM)] + [vmem] * 10,
        out_specs=(vmem, vmem),
        scratch_shapes=[pltpu.VMEM((3, B, 2 * B), F32)],
        compiler_params=pltpu.CompilerParams(vmem_limit_bytes=40 * 2**20),
        cost_estimate=pl.CostEstimate(flops=3 * 10**9, bytes_accessed=10**7, transcendentals=0),
        name="solve_columns",
    )(place, v, x, *pieces)


def update_kernel(place_ref, *refs):
    zhi_hbm, zlo_hbm, diag_hbm, a_hbm, u_hbm, o_hbm, zhi_ref, zlo_ref, diag_ref, a_ref, u_ref, z_sem, a_sem, u_sem, o_sem = refs
    my_row, my_col = place_ref[0], place_ref[1]
    panel = my_col < 3
    u_copies = [pltpu.make_async_copy(u_hbm.at[y], u_ref.at[y], u_sem.at[y]) for y in range(4)]
    a_copies = [pltpu.make_async_copy(a_hbm.at[t], a_ref.at[t], a_sem.at[t]) for t in range(8)]
    o_copies = [pltpu.make_async_copy(a_ref.at[t], o_hbm.at[t], o_sem.at[t]) for t in range(8)]
    z_copies = [
        pltpu.make_async_copy(zhi_hbm, zhi_ref, z_sem.at[0]),
        pltpu.make_async_copy(zlo_hbm, zlo_ref, z_sem.at[1]),
        pltpu.make_async_copy(diag_hbm, diag_ref, z_sem.at[2]),
    ]
    for copy in z_copies:
        copy.start()
    for y in range(4):
        u_copies[y].start()
        a_copies[y].start()
        a_copies[y + 4].start()

    for copy in z_copies:
        copy.wait()
    for y in range(4):
        u_copies[y].wait()
        for t in (y, y + 4):
            i = t * 8 + my_row
            a_copies[t].wait()

            def write(u, change):
                for half in range(2):
                    at = pl.ds(2 * half + u, B, stride=4)
                    base = a_ref[t, at, :]
                    if u == 0:
                        base = jnp.where(panel, 0.0, base)
                    a_ref[t, at, :] = base - change[:, half * 128 : half * 128 + 128]

            def turned():
                return split(u_ref[y, :, t // 4 * B : t // 4 * B + B].T)

            def left():
                write(0, product(turned(), (zhi_ref[:, :B], zlo_ref[:, :B])))

            if t < 4:
                pl.when(i >= my_col)(left)

                @pl.when(jnp.logical_and(i == my_col, panel))
                def _():
                    for half in range(2):
                        a_ref[t, pl.ds(2 * half, B, stride=4), :] = diag_ref[:, half * 128 : half * 128 + 128]
            else:
                both = i >= my_col + 32

                @pl.when(both)
                def _():
                    change = product(turned(), (zhi_ref[...], zlo_ref[...]))
                    write(0, change[:, :B])
                    write(1, change[:, B:])

                pl.when(jnp.logical_not(both))(left)
            o_copies[t].start()
    for t in range(8):
        o_copies[t].wait()


def update(place, a, u, zhi, zlo, diag):
    hbm = pl.BlockSpec(memory_space=pltpu.HBM)
    tiles, cols = a.shape[0], a.shape[2]
    flat = a.reshape(tiles, B, cols, 2, 128).transpose(0, 1, 3, 2, 4).reshape(tiles, 4 * B, 128)
    out = pl.pallas_call(
        update_kernel,
        out_shape=jax.ShapeDtypeStruct(flat.shape, F32),
        in_specs=[pl.BlockSpec(memory_space=pltpu.SMEM)] + [hbm] * 5,
        out_specs=hbm,
        scratch_shapes=[
            pltpu.VMEM((3 * B, 2 * B), BF16),
            pltpu.VMEM((3 * B, 2 * B), BF16),
            pltpu.VMEM((B, B), F32),
            pltpu.VMEM((8, 4 * B, 128), F32),
            pltpu.VMEM((4, 3 * B, 2 * B), F32),
            pltpu.SemaphoreType.DMA((3,)),
            pltpu.SemaphoreType.DMA((8,)),
            pltpu.SemaphoreType.DMA((4,)),
            pltpu.SemaphoreType.DMA((8,)),
        ],
        compiler_params=pltpu.CompilerParams(vmem_limit_bytes=58 * 2**20),
        cost_estimate=pl.CostEstimate(flops=5 * 10**9, bytes_accessed=14 * 10**6, transcendentals=0),
        name="trailing_update",
    )(place, zhi, zlo, diag, flat, u.reshape(4, 3 * B, 2 * B))
    return out.reshape(tiles, B, 2, cols, 128).transpose(0, 1, 3, 2, 4).reshape(a.shape)


def spread_corner(mine, my_col):
    y, z = my_col // 8, my_col % 8
    quarter = mine.reshape(3, 4, 8, B)
    got = jnp.where(y == 0, quarter[:, 0], 0.0)
    for d in range(1, 4):
        got = got + lax.ppermute(quarter[:, d], "col", [(j, d * 8 + j) for j in range(3)])
    got = jnp.where(z < 3, got, 0.0)
    got = got + lax.ppermute(got, "col", [(h * 8 + j, h * 8 + j + 4) for h in range(4) for j in range(3)])
    stack = [got]
    for s in range(1, 4):
        pairs = [
            (h * 8 + q * 4 + j, h * 8 + q * 4 + (j + s) % 4) for h in range(4) for q in range(2) for j in range(3)
        ]
        stack.append(lax.ppermute(got, "col", pairs))
    column = []
    for j in range(3):
        at = (z - j) % 4
        pick = stack[3]
        for s in range(3):
            pick = jnp.where(at == s, stack[s], pick)
        column.append(pick)
    part = jnp.stack([column[j][k] for k, j in PAIRS])
    parts = [part]
    for s in range(1, 4):
        parts.append(lax.ppermute(part, "col", [(c, (c + 8 * s) % 32) for c in range(32)]))
    block = jnp.stack(parts)
    own = [block]
    for s in range(1, 4):
        own.append(lax.ppermute(block, "row", [(r, (r + 2 * s) % 8) for r in range(8)]))
    other = [lax.ppermute(b, "row", [(r, r ^ 1) for r in range(8)]) for b in own]
    return own, other


def spread_columns(mine, after):
    mine, _ = lax.optimization_barrier((mine, after))
    pieces = []
    for n in range(8):
        pairs = [(r, (r // 2 + n // 2) % 4 * 2 + (r % 2) ^ (n % 2)) for r in range(8)]
        pieces.append(mine if n == 0 else lax.ppermute(mine, "row", pairs))
    return pieces


def on_device(covariance):
    my_row, my_col = lax.axis_index("row"), lax.axis_index("col")
    place = jnp.stack([my_row, my_col]).astype(jnp.int32)
    top = covariance[0].reshape(8, 32, 2 * B)
    mine = lax.all_to_all(top, "row", 0, 0, tiled=True)[:3]
    turned = lax.ppermute(
        mine,
        ("row", "col"),
        [(r * 32 + y * 8 + z, z * 32 + y * 8 + r) for r in range(8) for y in range(4) for z in range(8)],
    )
    rows = lax.all_gather(turned, "col")
    own, other = spread_corner(mine[:, :, :B], my_col)
    pieces = spread_columns(mine, own)
    v, x, diag = factor(place, own, other)
    zhi, zlo = solve(place, v, x, pieces)
    return update(place, covariance, rows, zhi, zlo, diag)


def solution(mesh):
    spec = (P(None, "row", None, "col"),)
    return jax.shard_map(on_device, mesh=mesh, in_specs=spec, out_specs=spec[0], check_vma=False)
```

```python
import functools

import jax
import jax.numpy as jnp
from jax import lax
from jax.experimental import pallas as pl
from jax.experimental.pallas import tpu as pltpu
from jax.sharding import PartitionSpec as P

B = 256
BAND = 32
PIV = 8
PAIRS = tuple((k, j) for k in range(3) for j in range(k, 3))
HIGHEST = lax.Precision.HIGHEST
F32 = jnp.float32
BF16 = jnp.bfloat16


def dot(a, b):
    return jnp.dot(a, b, precision=HIGHEST, preferred_element_type=F32)


def dot_tn(a, b):
    return lax.dot_general(
        a, b, (((0,), (0,)), ((), ())), precision=HIGHEST, preferred_element_type=F32
    )


def split(a):
    hi = a.astype(BF16)
    return hi, (a - hi.astype(F32)).astype(BF16)


def product(a, b):
    mul = functools.partial(jnp.dot, preferred_element_type=F32)
    return mul(a[0], b[0]) + (mul(a[0], b[1]) + mul(a[1], b[0]))


def band_eliminate(rows, band):
    iota = lax.broadcasted_iota(jnp.int32, (8, 128), 0)
    chunks = list(rows[0].keys())
    groups = BAND // 8
    for g in range(0, BAND, PIV):
        mine, first = g // 8, g % 8
        col = band * BAND + g
        piv_chunk, lane = col // 128, col % 128
        v = [
            [
                jnp.broadcast_to(rows[s][piv_chunk][:, lane + a : lane + a + 1], (8, 128)) if s >= mine else None
                for s in range(groups)
            ]
            for a in range(PIV)
        ]
        row = [
            {c: jnp.broadcast_to(rows[mine][c][first + a : first + a + 1, :], (8, 128)) for c in chunks}
            for a in range(PIV)
        ]
        s = {
            (a, b): jnp.broadcast_to(v[b][mine][first + a : first + a + 1, :], (8, 128))
            for a in range(PIV)
            for b in range(a, PIV)
        }
        inv, root = [], []
        for a in range(PIV):
            inv.append(1.0 / s[a, a])
            root.append(lax.rsqrt(s[a, a]))
            for b in range(a + 1, PIV):
                ratio = s[a, b] * inv[a]
                for c in range(b, PIV):
                    s[b, c] = s[b, c] - ratio * s[a, c]
                for c in chunks:
                    row[b][c] = row[b][c] - ratio * row[a][c]
                for h in range(mine, groups):
                    v[b][h] = v[b][h] - ratio * v[a][h]
        for h in range(mine, groups):
            if h == mine and first + PIV == 8:
                continue
            scaled = [v[a][h] * inv[a] for a in range(PIV)]
            for c in chunks:
                total = scaled[0] * row[0][c]
                for a in range(1, PIV):
                    total = total + scaled[a] * row[a][c]
                new = rows[h][c] - total
                rows[h][c] = jnp.where(iota >= first + PIV, new, rows[h][c]) if h == mine else new
        for a in range(PIV):
            for c in chunks:
                rows[mine][c] = jnp.where(iota == first + a, row[a][c] * root[a], rows[mine][c])
    return rows


def factor_tile(g_ref):
    for band in range(B // BAND):
        lo = band * BAND
        chunks = (0, 1, 2) if lo < 128 else (1, 2, 3)
        rows = [
            {c: g_ref[lo + 8 * s : lo + 8 * s + 8, 128 * c : 128 * c + 128] for c in chunks}
            for s in range(BAND // 8)
        ]
        rows = band_eliminate(rows, band)
        for s in range(BAND // 8):
            for c in chunks:
                g_ref[lo + 8 * s : lo + 8 * s + 8, 128 * c : 128 * c + 128] = rows[s][c]
        hi = lo + BAND
        if hi < B:
            left, right = 128 * chunks[0], 128 * chunks[-1] + 128
            done = g_ref[lo:hi, left:right]
            turned = g_ref[lo:hi, 0:B].T
            g_ref[hi : hi + BAND, left:right] -= dot(turned[hi : hi + BAND], done)
            if hi + BAND < B:
                g_ref[hi + BAND : B, left:right] -= dot(turned[hi + BAND : B], done)


def upper_mask():
    return lax.broadcasted_iota(jnp.int32, (B, B), 0) <= lax.broadcasted_iota(jnp.int32, (B, B), 1)


def unit():
    rows = lax.broadcasted_iota(jnp.int32, (B, B), 0)
    return jnp.where(rows == lax.broadcasted_iota(jnp.int32, (B, B), 1), 1.0, 0.0).astype(F32)


def factor_kernel(place_ref, *refs):
    own, other = refs[0:4], refs[4:8]
    v_ref, x_ref, diag_ref, t_ref, g_ref, lt_ref = refs[8:]
    my_row, my_col = place_ref[0], place_ref[1]
    x, core = my_row // 2, my_row % 2
    y = my_col // 8
    for shift in range(4):
        for side, bufs in ((core, own), (1 - core, other)):
            base = (((x - shift + 4) % 4) * 2 + side) * 32
            for step in range(4):
                at = pl.multiple_of(base + ((y - step + 4) % 4) * 8, 8)
                for n, (k, j) in enumerate(PAIRS):
                    t_ref[k, pl.ds(at, 8), j * B : (j + 1) * B] = bufs[shift][step, n]

    def step(k, carry):
        for j in range(3):

            @pl.when(k == j)
            def _():
                g_ref[:, 0:B] = t_ref[j, :, j * B : (j + 1) * B]

        g_ref[:, B:] = unit()
        factor_tile(g_ref)
        lt_ref[k] = jnp.where(upper_mask(), g_ref[:, 0:B], 0.0)
        v_ref[k] = g_ref[:, B:]
        for j in range(2):

            @pl.when(k == j)
            def _():
                lo = (j + 1) * B
                solved = dot(v_ref[j], t_ref[j, :, lo:])
                t_ref[j, :, lo:] = solved
                for i in range(j + 1, 3):
                    t_ref[i, :, i * B :] -= dot_tn(
                        t_ref[j, :, i * B : (i + 1) * B], t_ref[j, :, i * B :]
                    )

        return carry

    lax.fori_loop(0, 3, step, 0)
    for n, (k, j) in enumerate(((0, 1), (0, 2), (1, 2))):
        x_ref[n] = t_ref[k, :, j * B : (j + 1) * B]
    diag_ref[...] = lt_ref[jnp.minimum(my_col, 2)].T


def factor(place, own, other):
    vmem = pl.BlockSpec(memory_space=pltpu.VMEM)
    return pl.pallas_call(
        factor_kernel,
        out_shape=(
            jax.ShapeDtypeStruct((3, B, B), F32),
            jax.ShapeDtypeStruct((3, B, B), F32),
            jax.ShapeDtypeStruct((B, B), F32),
        ),
        in_specs=[pl.BlockSpec(memory_space=pltpu.SMEM)] + [vmem] * 8,
        out_specs=(vmem, vmem, vmem),
        scratch_shapes=[
            pltpu.VMEM((3, B, 3 * B), F32),
            pltpu.VMEM((B, 2 * B), F32),
            pltpu.VMEM((3, B, B), F32),
        ],
        compiler_params=pltpu.CompilerParams(vmem_limit_bytes=40 * 2**20),
        cost_estimate=pl.CostEstimate(flops=30 * 10**9, bytes_accessed=10**7, transcendentals=0),
        name="factor_corner",
    )(place, *own, *other)


def solve_kernel(place_ref, v_ref, x_ref, *refs):
    pieces = refs[:8]
    zhi_ref, zlo_ref, t_ref = refs[8:]
    my_row, my_col = place_ref[0], place_ref[1]
    x, core = my_row // 2, my_row % 2
    for n in range(8):
        source = ((x - n // 2 + 4) % 4) * 2 + (core if n % 2 == 0 else 1 - core)
        at = pl.multiple_of(source * 32, 32)
        for k in range(3):
            t_ref[k, pl.ds(at, 32), :] = pieces[n][k]
    above = {(0, 1): 0, (0, 2): 1, (1, 2): 2}
    v = [split(v_ref[k]) for k in range(3)]
    vt = [split(v_ref[k].T) for k in range(3)]
    up = {key: split(x_ref[n]) for key, n in above.items()}
    down = {key: split(x_ref[n].T) for key, n in above.items()}
    sums = [t_ref[k] for k in range(3)]
    for k in range(3):
        sums[k] = product(v[k], split(sums[k]))
        for i in range(k + 1, 3):
            sums[i] = sums[i] - product(down[k, i], split(sums[k]))
    for k in range(3):
        left = jnp.where(my_col == k, -unit(), jnp.where(my_col < 3, 0.0, sums[k][:, :B]))
        sums[k] = jnp.concatenate([left, sums[k][:, B:]], axis=1)
    done = [None] * 3
    for k in (2, 1, 0):
        rest = sums[k]
        for i in range(k + 1, 3):
            rest = rest - product(up[k, i], done[i])
        done[k] = split(product(vt[k], split(rest)))
        for ref, part in ((zhi_ref, done[k][0]), (zlo_ref, done[k][1])):
            for p in range(8):
                ref[p * 96 + k * 32 : p * 96 + k * 32 + 32, :] = part[p * 32 : p * 32 + 32]


def solve(place, v, x, pieces):
    vmem = pl.BlockSpec(memory_space=pltpu.VMEM)
    return pl.pallas_call(
        solve_kernel,
        out_shape=(
            jax.ShapeDtypeStruct((3 * B, 2 * B), BF16),
            jax.ShapeDtypeStruct((3 * B, 2 * B), BF16),
        ),
        in_specs=[pl.BlockSpec(memory_space=pltpu.SMEM)] + [vmem] * 10,
        out_specs=(vmem, vmem),
        scratch_shapes=[pltpu.VMEM((3, B, 2 * B), F32)],
        compiler_params=pltpu.CompilerParams(vmem_limit_bytes=40 * 2**20),
        cost_estimate=pl.CostEstimate(flops=3 * 10**9, bytes_accessed=10**7, transcendentals=0),
        name="solve_columns",
    )(place, v, x, *pieces)


def update_kernel(place_ref, *refs):
    zhi_ref, zlo_ref, diag_ref, a_hbm, u_hbm, o_hbm, a_ref, u_ref, a_sem, u_sem, o_sem = refs
    my_row, my_col = place_ref[0], place_ref[1]
    panel = my_col < 3
    u_copies = [pltpu.make_async_copy(u_hbm.at[y], u_ref.at[y], u_sem.at[y]) for y in range(4)]
    a_copies = [pltpu.make_async_copy(a_hbm.at[t], a_ref.at[t], a_sem.at[t]) for t in range(8)]
    o_copies = [pltpu.make_async_copy(a_ref.at[t], o_hbm.at[t], o_sem.at[t]) for t in range(8)]

    def fetch(y):
        u_copies[y].start()
        a_copies[y].start()
        a_copies[y + 4].start()

    fetch(0)
    fetch(1)
    for y in range(4):
        u_copies[y].wait()
        if y < 2:
            fetch(y + 2)
        for t in (y, y + 4):
            i = t * 8 + my_row
            a_copies[t].wait()

            def write(u, change):
                for half in range(2):
                    at = pl.ds(2 * half + u, B, stride=4)
                    base = a_ref[t, at, :]
                    if u == 0:
                        base = jnp.where(panel, 0.0, base)
                    a_ref[t, at, :] = base - change[:, half * 128 : half * 128 + 128]

            def turned():
                return split(u_ref[y, :, t // 4 * B : t // 4 * B + B].T)

            def left():
                write(0, product(turned(), (zhi_ref[:, :B], zlo_ref[:, :B])))

            if t < 4:
                pl.when(i >= my_col)(left)

                @pl.when(jnp.logical_and(i == my_col, panel))
                def _():
                    for half in range(2):
                        a_ref[t, pl.ds(2 * half, B, stride=4), :] = diag_ref[:, half * 128 : half * 128 + 128]
            else:
                both = i >= my_col + 32

                @pl.when(both)
                def _():
                    change = product(turned(), (zhi_ref[...], zlo_ref[...]))
                    write(0, change[:, :B])
                    write(1, change[:, B:])

                pl.when(jnp.logical_not(both))(left)
            o_copies[t].start()
    for t in range(8):
        o_copies[t].wait()


def update(place, a, u, zhi, zlo, diag):
    vmem = pl.BlockSpec(memory_space=pltpu.VMEM)
    hbm = pl.BlockSpec(memory_space=pltpu.HBM)
    tiles, cols = a.shape[0], a.shape[2]
    flat = a.reshape(tiles, B, cols, 2, 128).transpose(0, 1, 3, 2, 4).reshape(tiles, 4 * B, 128)
    out = pl.pallas_call(
        update_kernel,
        out_shape=jax.ShapeDtypeStruct(flat.shape, F32),
        in_specs=[pl.BlockSpec(memory_space=pltpu.SMEM), vmem, vmem, vmem, hbm, hbm],
        out_specs=hbm,
        scratch_shapes=[
            pltpu.VMEM((8, 4 * B, 128), F32),
            pltpu.VMEM((4, 3 * B, 2 * B), F32),
            pltpu.SemaphoreType.DMA((8,)),
            pltpu.SemaphoreType.DMA((4,)),
            pltpu.SemaphoreType.DMA((8,)),
        ],
        compiler_params=pltpu.CompilerParams(vmem_limit_bytes=49 * 2**20),
        cost_estimate=pl.CostEstimate(flops=5 * 10**9, bytes_accessed=14 * 10**6, transcendentals=0),
        name="trailing_update",
    )(place, zhi, zlo, diag, flat, u.reshape(4, 3 * B, 2 * B))
    return out.reshape(tiles, B, 2, cols, 128).transpose(0, 1, 3, 2, 4).reshape(a.shape)


def spread_corner(mine, my_col):
    y, z = my_col // 8, my_col % 8
    quarter = mine.reshape(3, 4, 8, B)
    got = jnp.where(y == 0, quarter[:, 0], 0.0)
    for d in range(1, 4):
        got = got + lax.ppermute(quarter[:, d], "col", [(j, d * 8 + j) for j in range(3)])
    got = jnp.where(z < 3, got, 0.0)
    first = got
    got = got + lax.ppermute(got, "col", [(h * 8 + j, h * 8 + j + 4) for h in range(4) for j in range(3)])
    stack = [got]
    for s in range(1, 4):
        pairs = [
            (h * 8 + q * 4 + j, h * 8 + q * 4 + (j + s) % 4) for h in range(4) for q in range(2) for j in range(3)
        ]
        stack.append(lax.ppermute(got, "col", pairs))
    column = []
    for j in range(3):
        at = (z - j) % 4
        pick = stack[3]
        for s in range(3):
            pick = jnp.where(at == s, stack[s], pick)
        column.append(pick)
    part = jnp.stack([column[j][k] for k, j in PAIRS])
    parts = [part]
    for s in range(1, 4):
        parts.append(lax.ppermute(part, "col", [(c, (c + 8 * s) % 32) for c in range(32)]))
    block = jnp.stack(parts)
    own = [block]
    for s in range(1, 4):
        own.append(lax.ppermute(block, "row", [(r, (r + 2 * s) % 8) for r in range(8)]))
    other = [lax.ppermute(b, "row", [(r, r ^ 1) for r in range(8)]) for b in own]
    return own, other, first


def spread_columns(mine, after):
    mine, _ = lax.optimization_barrier((mine, after))
    pieces = []
    for n in range(8):
        pairs = [(r, (r // 2 + n // 2) % 4 * 2 + (r % 2) ^ (n % 2)) for r in range(8)]
        pieces.append(mine if n == 0 else lax.ppermute(mine, "row", pairs))
    return pieces


def on_device(covariance):
    my_row, my_col = lax.axis_index("row"), lax.axis_index("col")
    place = jnp.stack([my_row, my_col]).astype(jnp.int32)
    top = covariance[0].reshape(8, 32, 2 * B)
    mine = lax.all_to_all(top, "row", 0, 0, tiled=True)[:3]
    turned = lax.ppermute(
        mine,
        ("row", "col"),
        [(r * 32 + y * 8 + z, z * 32 + y * 8 + r) for r in range(8) for y in range(4) for z in range(8)],
    )
    rows = lax.all_gather(turned, "col")
    own, other, first = spread_corner(mine[:, :, :B], my_col)
    pieces = spread_columns(mine, first)
    v, x, diag = factor(place, own, other)
    zhi, zlo = solve(place, v, x, pieces)
    return update(place, covariance, rows, zhi, zlo, diag)


def solution(mesh):
    spec = (P(None, "row", None, "col"),)
    return jax.shard_map(on_device, mesh=mesh, in_specs=spec, out_specs=spec[0], check_vma=False)
```

```python
import functools

import jax
import jax.numpy as jnp
from jax import lax
from jax.experimental import pallas as pl
from jax.experimental.pallas import tpu as pltpu
from jax.sharding import PartitionSpec as P

B = 256
BAND = 32
PIV = 8
PAIRS = tuple((k, j) for k in range(3) for j in range(k, 3))
SHIFT = (0, 4, 1, 7, 2, 6, 3, 5)
HIGHEST = lax.Precision.HIGHEST
F32 = jnp.float32
BF16 = jnp.bfloat16


def dot(a, b):
    return jnp.dot(a, b, precision=HIGHEST, preferred_element_type=F32)


def dot_tn(a, b):
    return lax.dot_general(
        a, b, (((0,), (0,)), ((), ())), precision=HIGHEST, preferred_element_type=F32
    )


def split(a):
    hi = a.astype(BF16)
    return hi, (a - hi.astype(F32)).astype(BF16)


def product(a, b):
    mul = functools.partial(jnp.dot, preferred_element_type=F32)
    return mul(a[0], b[0]) + (mul(a[0], b[1]) + mul(a[1], b[0]))


def band_eliminate(rows, band):
    iota = lax.broadcasted_iota(jnp.int32, (8, 128), 0)
    chunks = list(rows[0].keys())
    groups = BAND // 8
    for g in range(0, BAND, PIV):
        mine, first = g // 8, g % 8
        col = band * BAND + g
        piv_chunk, lane = col // 128, col % 128
        v = [
            [
                jnp.broadcast_to(rows[s][piv_chunk][:, lane + a : lane + a + 1], (8, 128)) if s >= mine else None
                for s in range(groups)
            ]
            for a in range(PIV)
        ]
        row = [
            {c: jnp.broadcast_to(rows[mine][c][first + a : first + a + 1, :], (8, 128)) for c in chunks}
            for a in range(PIV)
        ]
        s = {
            (a, b): jnp.broadcast_to(v[b][mine][first + a : first + a + 1, :], (8, 128))
            for a in range(PIV)
            for b in range(a, PIV)
        }
        inv, root = [], []
        for a in range(PIV):
            inv.append(1.0 / s[a, a])
            root.append(lax.rsqrt(s[a, a]))
            for b in range(a + 1, PIV):
                ratio = s[a, b] * inv[a]
                for c in range(b, PIV):
                    s[b, c] = s[b, c] - ratio * s[a, c]
                for c in chunks:
                    row[b][c] = row[b][c] - ratio * row[a][c]
                for h in range(mine, groups):
                    v[b][h] = v[b][h] - ratio * v[a][h]
        for h in range(mine, groups):
            if h == mine and first + PIV == 8:
                continue
            scaled = [v[a][h] * inv[a] for a in range(PIV)]
            for c in chunks:
                total = scaled[0] * row[0][c]
                for a in range(1, PIV):
                    total = total + scaled[a] * row[a][c]
                new = rows[h][c] - total
                rows[h][c] = jnp.where(iota >= first + PIV, new, rows[h][c]) if h == mine else new
        for a in range(PIV):
            for c in chunks:
                rows[mine][c] = jnp.where(iota == first + a, row[a][c] * root[a], rows[mine][c])
    return rows


def factor_tile(g_ref):
    for band in range(B // BAND):
        lo = band * BAND
        chunks = (0, 1, 2) if lo < 128 else (1, 2, 3)
        rows = [
            {c: g_ref[lo + 8 * s : lo + 8 * s + 8, 128 * c : 128 * c + 128] for c in chunks}
            for s in range(BAND // 8)
        ]
        rows = band_eliminate(rows, band)
        for s in range(BAND // 8):
            for c in chunks:
                g_ref[lo + 8 * s : lo + 8 * s + 8, 128 * c : 128 * c + 128] = rows[s][c]
        hi = lo + BAND
        if hi < B:
            left, right = 128 * chunks[0], 128 * chunks[-1] + 128
            done = g_ref[lo:hi, left:right]
            turned = g_ref[lo:hi, 0:B].T
            g_ref[hi : hi + BAND, left:right] -= dot(turned[hi : hi + BAND], done)
            if hi + BAND < B:
                g_ref[hi + BAND : B, left:right] -= dot(turned[hi + BAND : B], done)


def upper_mask():
    return lax.broadcasted_iota(jnp.int32, (B, B), 0) <= lax.broadcasted_iota(jnp.int32, (B, B), 1)


def unit():
    rows = lax.broadcasted_iota(jnp.int32, (B, B), 0)
    return jnp.where(rows == lax.broadcasted_iota(jnp.int32, (B, B), 1), 1.0, 0.0).astype(F32)


def factor_kernel(place_ref, *refs):
    own, other = refs[0:4], refs[4:8]
    v_ref, x_ref, diag_ref, t_ref, g_ref, lt_ref = refs[8:]
    my_row, my_col = place_ref[0], place_ref[1]
    x, core = my_row // 2, my_row % 2
    y = my_col // 8
    for shift in range(4):
        for side, bufs in ((core, own), (1 - core, other)):
            base = (((x - shift + 4) % 4) * 2 + side) * 32
            for step in range(4):
                at = pl.multiple_of(base + ((y - step + 4) % 4) * 8, 8)
                for n, (k, j) in enumerate(PAIRS):
                    t_ref[k, pl.ds(at, 8), j * B : (j + 1) * B] = bufs[shift][step, n]

    def step(k, carry):
        for j in range(3):

            @pl.when(k == j)
            def _():
                g_ref[:, 0:B] = t_ref[j, :, j * B : (j + 1) * B]

        g_ref[:, B:] = unit()
        factor_tile(g_ref)
        lt_ref[k] = jnp.where(upper_mask(), g_ref[:, 0:B], 0.0)
        v_ref[k] = g_ref[:, B:]
        for j in range(2):

            @pl.when(k == j)
            def _():
                lo = (j + 1) * B
                solved = dot(v_ref[j], t_ref[j, :, lo:])
                t_ref[j, :, lo:] = solved
                for i in range(j + 1, 3):
                    t_ref[i, :, i * B :] -= dot_tn(
                        t_ref[j, :, i * B : (i + 1) * B], t_ref[j, :, i * B :]
                    )

        return carry

    lax.fori_loop(0, 3, step, 0)
    for n, (k, j) in enumerate(((0, 1), (0, 2), (1, 2))):
        x_ref[n] = t_ref[k, :, j * B : (j + 1) * B]
    diag_ref[...] = lt_ref[jnp.minimum(my_col, 2)].T


def factor(place, own, other):
    vmem = pl.BlockSpec(memory_space=pltpu.VMEM)
    return pl.pallas_call(
        factor_kernel,
        out_shape=(
            jax.ShapeDtypeStruct((3, B, B), F32),
            jax.ShapeDtypeStruct((3, B, B), F32),
            jax.ShapeDtypeStruct((B, B), F32),
        ),
        in_specs=[pl.BlockSpec(memory_space=pltpu.SMEM)] + [vmem] * 8,
        out_specs=(vmem, vmem, vmem),
        scratch_shapes=[
            pltpu.VMEM((3, B, 3 * B), F32),
            pltpu.VMEM((B, 2 * B), F32),
            pltpu.VMEM((3, B, B), F32),
        ],
        compiler_params=pltpu.CompilerParams(vmem_limit_bytes=40 * 2**20),
        cost_estimate=pl.CostEstimate(flops=30 * 10**9, bytes_accessed=10**7, transcendentals=0),
        name="factor_corner",
    )(place, *own, *other)


def solve_kernel(place_ref, v_ref, x_ref, *refs):
    pieces = refs[:8]
    zhi_ref, zlo_ref, t_ref = refs[8:]
    my_row, my_col = place_ref[0], place_ref[1]
    x, core = my_row // 2, my_row % 2
    for n in range(8):
        source = ((x - n // 2 + 4) % 4) * 2 + (core if n % 2 == 0 else 1 - core)
        at = pl.multiple_of(source * 32, 32)
        for k in range(3):
            t_ref[k, pl.ds(at, 32), :] = pieces[n][k]
    above = {(0, 1): 0, (0, 2): 1, (1, 2): 2}
    v = [split(v_ref[k]) for k in range(3)]
    vt = [split(v_ref[k].T) for k in range(3)]
    up = {key: split(x_ref[n]) for key, n in above.items()}
    down = {key: split(x_ref[n].T) for key, n in above.items()}
    sums = [t_ref[k] for k in range(3)]
    for k in range(3):
        sums[k] = product(v[k], split(sums[k]))
        for i in range(k + 1, 3):
            sums[i] = sums[i] - product(down[k, i], split(sums[k]))
    for k in range(3):
        left = jnp.where(my_col == k, -unit(), jnp.where(my_col < 3, 0.0, sums[k][:, :B]))
        sums[k] = jnp.concatenate([left, sums[k][:, B:]], axis=1)
    done = [None] * 3
    for k in (2, 1, 0):
        rest = sums[k]
        for i in range(k + 1, 3):
            rest = rest - product(up[k, i], done[i])
        done[k] = split(product(vt[k], split(rest)))
        for ref, part in ((zhi_ref, done[k][0]), (zlo_ref, done[k][1])):
            for p in range(8):
                to = pl.multiple_of((my_row + SHIFT[p]) % 8 * 96 + k * 32, 32)
                ref[pl.ds(to, 32), :] = part[p * 32 : p * 32 + 32]


def solve(place, v, x, pieces):
    vmem = pl.BlockSpec(memory_space=pltpu.VMEM)
    return pl.pallas_call(
        solve_kernel,
        out_shape=(
            jax.ShapeDtypeStruct((3 * B, 2 * B), BF16),
            jax.ShapeDtypeStruct((3 * B, 2 * B), BF16),
        ),
        in_specs=[pl.BlockSpec(memory_space=pltpu.SMEM)] + [vmem] * 10,
        out_specs=(vmem, vmem),
        scratch_shapes=[pltpu.VMEM((3, B, 2 * B), F32)],
        compiler_params=pltpu.CompilerParams(vmem_limit_bytes=40 * 2**20),
        cost_estimate=pl.CostEstimate(flops=3 * 10**9, bytes_accessed=10**7, transcendentals=0),
        name="solve_columns",
    )(place, v, x, *pieces)


def update_kernel(place_ref, *refs):
    zhi_ref, zlo_ref, diag_ref, a_hbm, u_hbm, o_hbm, a_ref, u_ref, a_sem, u_sem, o_sem = refs
    my_row, my_col = place_ref[0], place_ref[1]
    panel = my_col < 3
    u_copies = [pltpu.make_async_copy(u_hbm.at[y], u_ref.at[y], u_sem.at[y]) for y in range(4)]
    a_copies = [pltpu.make_async_copy(a_hbm.at[t], a_ref.at[t], a_sem.at[t]) for t in range(8)]
    o_copies = [pltpu.make_async_copy(a_ref.at[t], o_hbm.at[t], o_sem.at[t]) for t in range(8)]

    def fetch(y):
        u_copies[y].start()
        a_copies[y].start()
        a_copies[y + 4].start()

    fetch(0)
    fetch(1)
    for y in range(4):
        u_copies[y].wait()
        if y < 2:
            fetch(y + 2)
        for t in (y, y + 4):
            i = t * 8 + my_row
            a_copies[t].wait()

            def write(u, change):
                for half in range(2):
                    at = pl.ds(2 * half + u, B, stride=4)
                    base = a_ref[t, at, :]
                    if u == 0:
                        base = jnp.where(panel, 0.0, base)
                    a_ref[t, at, :] = base - change[:, half * 128 : half * 128 + 128]

            def turned():
                return split(u_ref[y, :, t // 4 * B : t // 4 * B + B].T)

            def left():
                write(0, product(turned(), (zhi_ref[:, :B], zlo_ref[:, :B])))

            if t < 4:
                pl.when(i >= my_col)(left)

                @pl.when(jnp.logical_and(i == my_col, panel))
                def _():
                    for half in range(2):
                        a_ref[t, pl.ds(2 * half, B, stride=4), :] = diag_ref[:, half * 128 : half * 128 + 128]
            else:
                both = i >= my_col + 32

                @pl.when(both)
                def _():
                    change = product(turned(), (zhi_ref[...], zlo_ref[...]))
                    write(0, change[:, :B])
                    write(1, change[:, B:])

                pl.when(jnp.logical_not(both))(left)
            o_copies[t].start()
    for t in range(8):
        o_copies[t].wait()


def update(place, a, u, zhi, zlo, diag):
    vmem = pl.BlockSpec(memory_space=pltpu.VMEM)
    hbm = pl.BlockSpec(memory_space=pltpu.HBM)
    tiles, cols = a.shape[0], a.shape[2]
    flat = a.reshape(tiles, B, cols, 2, 128).transpose(0, 1, 3, 2, 4).reshape(tiles, 4 * B, 128)
    out = pl.pallas_call(
        update_kernel,
        out_shape=jax.ShapeDtypeStruct(flat.shape, F32),
        in_specs=[pl.BlockSpec(memory_space=pltpu.SMEM), vmem, vmem, vmem, hbm, hbm],
        out_specs=hbm,
        scratch_shapes=[
            pltpu.VMEM((8, 4 * B, 128), F32),
            pltpu.VMEM((4, 3 * B, 2 * B), F32),
            pltpu.SemaphoreType.DMA((8,)),
            pltpu.SemaphoreType.DMA((4,)),
            pltpu.SemaphoreType.DMA((8,)),
        ],
        compiler_params=pltpu.CompilerParams(vmem_limit_bytes=49 * 2**20),
        cost_estimate=pl.CostEstimate(flops=5 * 10**9, bytes_accessed=14 * 10**6, transcendentals=0),
        name="trailing_update",
    )(place, zhi, zlo, diag, flat, u.reshape(4, 3 * B, 2 * B))
    return out.reshape(tiles, B, 2, cols, 128).transpose(0, 1, 3, 2, 4).reshape(a.shape)


def spread_corner(mine, my_col):
    y, z = my_col // 8, my_col % 8
    quarter = mine.reshape(3, 4, 8, B)
    got = jnp.where(y == 0, quarter[:, 0], 0.0)
    for d in range(1, 4):
        got = got + lax.ppermute(quarter[:, d], "col", [(j, d * 8 + j) for j in range(3)])
    got = jnp.where(z < 3, got, 0.0)
    first = got
    got = got + lax.ppermute(got, "col", [(h * 8 + j, h * 8 + j + 4) for h in range(4) for j in range(3)])
    stack = [got]
    for s in range(1, 4):
        pairs = [
            (h * 8 + q * 4 + j, h * 8 + q * 4 + (j + s) % 4) for h in range(4) for q in range(2) for j in range(3)
        ]
        stack.append(lax.ppermute(got, "col", pairs))
    column = []
    for j in range(3):
        at = (z - j) % 4
        pick = stack[3]
        for s in range(3):
            pick = jnp.where(at == s, stack[s], pick)
        column.append(pick)
    part = jnp.stack([column[j][k] for k, j in PAIRS])
    parts = [part]
    for s in range(1, 4):
        parts.append(lax.ppermute(part, "col", [(c, (c + 8 * s) % 32) for c in range(32)]))
    block = jnp.stack(parts)
    own = [block]
    for s in range(1, 4):
        own.append(lax.ppermute(block, "row", [(r, (r + 2 * s) % 8) for r in range(8)]))
    other = [lax.ppermute(b, "row", [(r, r ^ 1) for r in range(8)]) for b in own]
    return own, other, first


def spread_columns(mine, after):
    mine, _ = lax.optimization_barrier((mine, after))
    pieces = []
    for n in range(8):
        pairs = [(r, (r // 2 + n // 2) % 4 * 2 + (r % 2) ^ (n % 2)) for r in range(8)]
        pieces.append(mine if n == 0 else lax.ppermute(mine, "row", pairs))
    return pieces


def on_device(covariance):
    my_row, my_col = lax.axis_index("row"), lax.axis_index("col")
    place = jnp.stack([my_row, my_col]).astype(jnp.int32)
    top = covariance[0].reshape(8, 32, 2 * B)
    mine = lax.all_to_all(top, "row", 0, 0, tiled=True)[:3]
    places = [(r, y, z) for r in range(8) for y in range(4) for z in range(8)]
    turned = lax.ppermute(
        mine, ("row", "col"), [(r * 32 + y * 8 + z, z * 32 + y * 8 + (z + SHIFT[r]) % 8) for r, y, z in places]
    )
    rows = lax.all_gather(turned, "col")
    own, other, first = spread_corner(mine[:, :, :B], my_col)
    pieces = spread_columns(mine, first)
    v, x, diag = factor(place, own, other)
    zhi, zlo = solve(place, v, x, pieces)
    return update(place, covariance, rows, zhi, zlo, diag)


def solution(mesh):
    spec = (P(None, "row", None, "col"),)
    return jax.shard_map(on_device, mesh=mesh, in_specs=spec, out_specs=spec[0], check_vma=False)
```

```python
import functools

import jax
import jax.numpy as jnp
from jax import lax
from jax.experimental import pallas as pl
from jax.experimental.pallas import tpu as pltpu
from jax.sharding import PartitionSpec as P

B = 256
BAND = 32
PIV = 8
PAIRS = tuple((k, j) for k in range(3) for j in range(k, 3))
SHIFT = (0, 4, 1, 7, 2, 6, 3, 5)
HIGHEST = lax.Precision.HIGHEST
F32 = jnp.float32
BF16 = jnp.bfloat16


def dot(a, b):
    return jnp.dot(a, b, precision=HIGHEST, preferred_element_type=F32)


def dot_tn(a, b):
    return lax.dot_general(
        a, b, (((0,), (0,)), ((), ())), precision=HIGHEST, preferred_element_type=F32
    )


def split(a):
    hi = a.astype(BF16)
    return hi, (a - hi.astype(F32)).astype(BF16)


def product(a, b):
    mul = functools.partial(jnp.dot, preferred_element_type=F32)
    return mul(a[0], b[0]) + (mul(a[0], b[1]) + mul(a[1], b[0]))


def band_eliminate(rows, band):
    iota = lax.broadcasted_iota(jnp.int32, (8, 128), 0)
    chunks = list(rows[0].keys())
    groups = BAND // 8
    for g in range(0, BAND, PIV):
        mine, first = g // 8, g % 8
        col = band * BAND + g
        piv_chunk, lane = col // 128, col % 128
        v = [
            [
                jnp.broadcast_to(rows[s][piv_chunk][:, lane + a : lane + a + 1], (8, 128)) if s >= mine else None
                for s in range(groups)
            ]
            for a in range(PIV)
        ]
        row = [
            {c: jnp.broadcast_to(rows[mine][c][first + a : first + a + 1, :], (8, 128)) for c in chunks}
            for a in range(PIV)
        ]
        s = {
            (a, b): jnp.broadcast_to(v[b][mine][first + a : first + a + 1, :], (8, 128))
            for a in range(PIV)
            for b in range(a, PIV)
        }
        inv, root = [], []
        for a in range(PIV):
            inv.append(1.0 / s[a, a])
            root.append(lax.rsqrt(s[a, a]))
            for b in range(a + 1, PIV):
                ratio = s[a, b] * inv[a]
                for c in range(b, PIV):
                    s[b, c] = s[b, c] - ratio * s[a, c]
                for c in chunks:
                    row[b][c] = row[b][c] - ratio * row[a][c]
                for h in range(mine, groups):
                    v[b][h] = v[b][h] - ratio * v[a][h]
        for h in range(mine, groups):
            if h == mine and first + PIV == 8:
                continue
            scaled = [v[a][h] * inv[a] for a in range(PIV)]
            for c in chunks:
                total = scaled[0] * row[0][c]
                for a in range(1, PIV):
                    total = total + scaled[a] * row[a][c]
                new = rows[h][c] - total
                rows[h][c] = jnp.where(iota >= first + PIV, new, rows[h][c]) if h == mine else new
        for a in range(PIV):
            for c in chunks:
                rows[mine][c] = jnp.where(iota == first + a, row[a][c] * root[a], rows[mine][c])
    return rows


def factor_tile(g_ref):
    for band in range(B // BAND):
        lo = band * BAND
        chunks = (0, 1, 2) if lo < 128 else (1, 2, 3)
        rows = [
            {c: g_ref[lo + 8 * s : lo + 8 * s + 8, 128 * c : 128 * c + 128] for c in chunks}
            for s in range(BAND // 8)
        ]
        rows = band_eliminate(rows, band)
        for s in range(BAND // 8):
            for c in chunks:
                g_ref[lo + 8 * s : lo + 8 * s + 8, 128 * c : 128 * c + 128] = rows[s][c]
        hi = lo + BAND
        if hi < B:
            left, right = 128 * chunks[0], 128 * chunks[-1] + 128
            done = g_ref[lo:hi, left:right]
            turned = g_ref[lo:hi, 0:B].T
            g_ref[hi : hi + BAND, left:right] -= dot(turned[hi : hi + BAND], done)
            if hi + BAND < B:
                g_ref[hi + BAND : B, left:right] -= dot(turned[hi + BAND : B], done)


def product_tn(a, b):
    mul = lambda p, q: lax.dot_general(p, q, (((0,), (0,)), ((), ())), preferred_element_type=F32)
    return mul(a[0], b[0]) + (mul(a[0], b[1]) + mul(a[1], b[0]))


def upper_mask():
    return lax.broadcasted_iota(jnp.int32, (B, B), 0) <= lax.broadcasted_iota(jnp.int32, (B, B), 1)


def unit():
    rows = lax.broadcasted_iota(jnp.int32, (B, B), 0)
    return jnp.where(rows == lax.broadcasted_iota(jnp.int32, (B, B), 1), 1.0, 0.0).astype(F32)


def factor_kernel(place_ref, *refs):
    own, other = refs[0:4], refs[4:8]
    v_ref, x_ref, diag_ref, t_ref, g_ref, lt_ref = refs[8:]
    my_row, my_col = place_ref[0], place_ref[1]
    x, core = my_row // 2, my_row % 2
    y = my_col // 8
    for shift in range(4):
        for side, bufs in ((core, own), (1 - core, other)):
            base = (((x - shift + 4) % 4) * 2 + side) * 32
            for step in range(4):
                at = pl.multiple_of(base + ((y - step + 4) % 4) * 8, 8)
                for n, (k, j) in enumerate(PAIRS):
                    t_ref[k, pl.ds(at, 8), j * B : (j + 1) * B] = bufs[shift][step, n]

    def step(k, carry):
        for j in range(3):

            @pl.when(k == j)
            def _():
                g_ref[:, 0:B] = t_ref[j, :, j * B : (j + 1) * B]

        g_ref[:, B:] = unit()
        factor_tile(g_ref)
        lt_ref[k] = jnp.where(upper_mask(), g_ref[:, 0:B], 0.0)
        v_ref[k] = g_ref[:, B:]
        for j in range(2):

            @pl.when(k == j)
            def _():
                lo = (j + 1) * B
                solved = dot(v_ref[j], t_ref[j, :, lo:])
                t_ref[j, :, lo:] = solved
                for i in range(j + 1, 3):
                    t_ref[i, :, i * B :] -= dot_tn(
                        t_ref[j, :, i * B : (i + 1) * B], t_ref[j, :, i * B :]
                    )

        return carry

    lax.fori_loop(0, 3, step, 0)
    for n, (k, j) in enumerate(((0, 1), (0, 2), (1, 2))):
        x_ref[n] = t_ref[k, :, j * B : (j + 1) * B]
    diag_ref[...] = lt_ref[jnp.minimum(my_col, 2)].T


def factor(place, own, other):
    vmem = pl.BlockSpec(memory_space=pltpu.VMEM)
    return pl.pallas_call(
        factor_kernel,
        out_shape=(
            jax.ShapeDtypeStruct((3, B, B), F32),
            jax.ShapeDtypeStruct((3, B, B), F32),
            jax.ShapeDtypeStruct((B, B), F32),
        ),
        in_specs=[pl.BlockSpec(memory_space=pltpu.SMEM)] + [vmem] * 8,
        out_specs=(vmem, vmem, vmem),
        scratch_shapes=[
            pltpu.VMEM((3, B, 3 * B), F32),
            pltpu.VMEM((B, 2 * B), F32),
            pltpu.VMEM((3, B, B), F32),
        ],
        compiler_params=pltpu.CompilerParams(vmem_limit_bytes=40 * 2**20),
        cost_estimate=pl.CostEstimate(flops=30 * 10**9, bytes_accessed=10**7, transcendentals=0),
        name="factor_corner",
    )(place, *own, *other)


def solve_kernel(place_ref, v_ref, x_ref, *refs):
    pieces = refs[:8]
    zhi_ref, zlo_ref, t_ref = refs[8:]
    my_row, my_col = place_ref[0], place_ref[1]
    x, core = my_row // 2, my_row % 2
    for n in range(8):
        source = ((x - n // 2 + 4) % 4) * 2 + (core if n % 2 == 0 else 1 - core)
        at = pl.multiple_of(source * 32, 32)
        for k in range(3):
            t_ref[k, pl.ds(at, 32), :] = pieces[n][k]
    above = {(0, 1): 0, (0, 2): 1, (1, 2): 2}
    v = [split(v_ref[k]) for k in range(3)]
    vt = [split(v_ref[k].T) for k in range(3)]
    up = {key: split(x_ref[n]) for key, n in above.items()}
    down = {key: split(x_ref[n].T) for key, n in above.items()}
    sums = [t_ref[k] for k in range(3)]
    for k in range(3):
        sums[k] = product(v[k], split(sums[k]))
        for i in range(k + 1, 3):
            sums[i] = sums[i] - product(down[k, i], split(sums[k]))
    for k in range(3):
        left = jnp.where(my_col == k, -unit(), jnp.where(my_col < 3, 0.0, sums[k][:, :B]))
        sums[k] = jnp.concatenate([left, sums[k][:, B:]], axis=1)
    done = [None] * 3
    for k in (2, 1, 0):
        rest = sums[k]
        for i in range(k + 1, 3):
            rest = rest - product(up[k, i], done[i])
        done[k] = split(product(vt[k], split(rest)))
        for ref, part in ((zhi_ref, done[k][0]), (zlo_ref, done[k][1])):
            for p in range(8):
                to = pl.multiple_of((my_row + SHIFT[p]) % 8 * 96 + k * 32, 32)
                ref[pl.ds(to, 32), :] = part[p * 32 : p * 32 + 32]


def solve(place, v, x, pieces):
    vmem = pl.BlockSpec(memory_space=pltpu.VMEM)
    return pl.pallas_call(
        solve_kernel,
        out_shape=(
            jax.ShapeDtypeStruct((3 * B, 2 * B), BF16),
            jax.ShapeDtypeStruct((3 * B, 2 * B), BF16),
        ),
        in_specs=[pl.BlockSpec(memory_space=pltpu.SMEM)] + [vmem] * 10,
        out_specs=(vmem, vmem),
        scratch_shapes=[pltpu.VMEM((3, B, 2 * B), F32)],
        compiler_params=pltpu.CompilerParams(vmem_limit_bytes=40 * 2**20),
        cost_estimate=pl.CostEstimate(flops=3 * 10**9, bytes_accessed=10**7, transcendentals=0),
        name="solve_columns",
    )(place, v, x, *pieces)


def update_kernel(place_ref, *refs):
    zhi_ref, zlo_ref, diag_ref, a_hbm, u_hbm, o_hbm, a_ref, u_ref, a_sem, u_sem, o_sem = refs
    my_row, my_col = place_ref[0], place_ref[1]
    panel = my_col < 3
    u_copies = []
    for t in range(8):
        part = (t % 4, slice(None), pl.ds(t // 4 * B, B))
        u_copies.append(pltpu.make_async_copy(u_hbm.at[part], u_ref.at[part], u_sem.at[t]))
    a_copies = [pltpu.make_async_copy(a_hbm.at[t], a_ref.at[t], a_sem.at[t]) for t in range(8)]
    o_copies = [pltpu.make_async_copy(a_ref.at[t], o_hbm.at[t], o_sem.at[t]) for t in range(8)]

    def fetch(y):
        for t in (y, y + 4):
            u_copies[t].start()
            a_copies[t].start()

    fetch(0)
    fetch(1)
    for y in range(4):
        for t in (y, y + 4):
            i = t * 8 + my_row
            u_copies[t].wait()
            if t < 2:
                fetch(t + 2)
            a_copies[t].wait()

            def write(u, change):
                for half in range(2):
                    at = pl.ds(2 * half + u, B, stride=4)
                    base = a_ref[t, at, :]
                    if u == 0:
                        base = jnp.where(panel, 0.0, base)
                    a_ref[t, at, :] = base - change[:, half * 128 : half * 128 + 128]

            def turned():
                return split(u_ref[y, :, t // 4 * B : t // 4 * B + B])

            def left():
                write(0, product_tn(turned(), (zhi_ref[:, :B], zlo_ref[:, :B])))

            if t < 4:
                pl.when(i >= my_col)(left)

                @pl.when(jnp.logical_and(i == my_col, panel))
                def _():
                    for half in range(2):
                        a_ref[t, pl.ds(2 * half, B, stride=4), :] = diag_ref[:, half * 128 : half * 128 + 128]
            else:
                both = i >= my_col + 32

                @pl.when(both)
                def _():
                    change = product_tn(turned(), (zhi_ref[...], zlo_ref[...]))
                    write(0, change[:, :B])
                    write(1, change[:, B:])

                pl.when(jnp.logical_not(both))(left)
            o_copies[t].start()
    for t in range(8):
        o_copies[t].wait()


def update(place, a, u, zhi, zlo, diag):
    vmem = pl.BlockSpec(memory_space=pltpu.VMEM)
    hbm = pl.BlockSpec(memory_space=pltpu.HBM)
    tiles, cols = a.shape[0], a.shape[2]
    flat = a.reshape(tiles, B, cols, 2, 128).transpose(0, 1, 3, 2, 4).reshape(tiles, 4 * B, 128)
    out = pl.pallas_call(
        update_kernel,
        out_shape=jax.ShapeDtypeStruct(flat.shape, F32),
        in_specs=[pl.BlockSpec(memory_space=pltpu.SMEM), vmem, vmem, vmem, hbm, hbm],
        out_specs=hbm,
        scratch_shapes=[
            pltpu.VMEM((8, 4 * B, 128), F32),
            pltpu.VMEM((4, 3 * B, 2 * B), F32),
            pltpu.SemaphoreType.DMA((8,)),
            pltpu.SemaphoreType.DMA((8,)),
            pltpu.SemaphoreType.DMA((8,)),
        ],
        compiler_params=pltpu.CompilerParams(vmem_limit_bytes=49 * 2**20),
        cost_estimate=pl.CostEstimate(flops=5 * 10**9, bytes_accessed=14 * 10**6, transcendentals=0),
        name="trailing_update",
    )(place, zhi, zlo, diag, flat, u.reshape(4, 3 * B, 2 * B))
    return out.reshape(tiles, B, 2, cols, 128).transpose(0, 1, 3, 2, 4).reshape(a.shape)


def spread_corner(mine, my_col):
    y, z = my_col // 8, my_col % 8
    quarter = mine.reshape(3, 4, 8, B)
    got = jnp.where(y == 0, quarter[:, 0], 0.0)
    for d in range(1, 4):
        got = got + lax.ppermute(quarter[:, d], "col", [(j, d * 8 + j) for j in range(3)])
    got = jnp.where(z < 3, got, 0.0)
    first = got
    got = got + lax.ppermute(got, "col", [(h * 8 + j, h * 8 + j + 4) for h in range(4) for j in range(3)])
    stack = [got]
    for s in range(1, 4):
        pairs = [
            (h * 8 + q * 4 + j, h * 8 + q * 4 + (j + s) % 4) for h in range(4) for q in range(2) for j in range(3)
        ]
        stack.append(lax.ppermute(got, "col", pairs))
    column = []
    for j in range(3):
        at = (z - j) % 4
        pick = stack[3]
        for s in range(3):
            pick = jnp.where(at == s, stack[s], pick)
        column.append(pick)
    part = jnp.stack([column[j][k] for k, j in PAIRS])
    parts = [part]
    for s in range(1, 4):
        parts.append(lax.ppermute(part, "col", [(c, (c + 8 * s) % 32) for c in range(32)]))
    block = jnp.stack(parts)
    own = [block]
    for s in range(1, 4):
        own.append(lax.ppermute(block, "row", [(r, (r + 2 * s) % 8) for r in range(8)]))
    other = [lax.ppermute(b, "row", [(r, r ^ 1) for r in range(8)]) for b in own]
    return own, other, first


def spread_columns(mine, after):
    mine, _ = lax.optimization_barrier((mine, after))
    pieces = []
    for n in range(8):
        pairs = [(r, (r // 2 + n // 2) % 4 * 2 + (r % 2) ^ (n % 2)) for r in range(8)]
        pieces.append(mine if n == 0 else lax.ppermute(mine, "row", pairs))
    return pieces


def on_device(covariance):
    my_row, my_col = lax.axis_index("row"), lax.axis_index("col")
    place = jnp.stack([my_row, my_col]).astype(jnp.int32)
    top = covariance[0].reshape(8, 32, 2 * B)
    mine = lax.all_to_all(top, "row", 0, 0, tiled=True)[:3]
    places = [(r, y, z) for r in range(8) for y in range(4) for z in range(8)]
    turned = lax.ppermute(
        mine, ("row", "col"), [(r * 32 + y * 8 + z, z * 32 + y * 8 + (z + SHIFT[r]) % 8) for r, y, z in places]
    )
    rows = lax.all_gather(turned, "col")
    own, other, first = spread_corner(mine[:, :, :B], my_col)
    pieces = spread_columns(mine, first)
    v, x, diag = factor(place, own, other)
    zhi, zlo = solve(place, v, x, pieces)
    return update(place, covariance, rows, zhi, zlo, diag)


def solution(mesh):
    spec = (P(None, "row", None, "col"),)
    return jax.shard_map(on_device, mesh=mesh, in_specs=spec, out_specs=spec[0], check_vma=False)
```
